256 devices in a mesh: row: 4 (over z_hi), col: 16 (over x, y), layer: 4 (over z_lo, core).
Axes of the slice: x: 4, y: 4, z: 8 (z_hi: 4, z_lo: 2; z = z_hi * 2 + z_lo), core: 2. Of those that a mesh axis runs over, the one named last changes fastest.
Arguments:
- a_tiles: bfloat16 [4, 4, 16, 8, 4096], P('row', 'layer', 'col'), may hold values from -6 to 6
- b_tiles: bfloat16 [4, 4, 16, 16, 4096], P('layer', 'row', 'col'), may hold values from -0.25 to 0.25
- a_slots: int32 [4, 16, 4, 768], P('row', 'col', 'layer'), may hold values from 0 to 128, as said below
- b_slots: int32 [4, 16, 4, 768], P('row', 'col', 'layer'), may hold values from 0 to 63, as said below
Outputs:
- c_tiles: bfloat16 [4, 16, 96, 4096], P('row', 'col', 'layer')
The draws below stay inside these ranges and needn't reach their ends.
Inputs may be any that keep to these rules, and one draw needn't show every extreme that they name: `a_slots`: entries s * 8 to s * 8 + 7 are the tasks of product tile s; the value 128 marks a dummy task (the zero tile); a tile's live tasks come first, every tile has at least 2 live tasks, and in every list some tile has 8 live tasks and some tile has dummies. `b_slots`: A dummy task holds 0 here.
All inputs are finite; a program needn't handle non-finite values.
Results may differ from the reference program's by a relative error of at most 0.013.
Values may be sent and summed in bfloat16 or wider, within the bound.
A program may use at most 128 MiB of HBM per device.

```python
import jax
import jax.numpy as jnp
from jax import lax

TILE = 64
TASKS = 8
TA = 8
TB = 16
TC = 96
N_ROW = 4
N_COL = 16
N_LAYER = 4


def live_entries(key):
    count_key, top_key, half_key = jax.random.split(key, 3)
    grid_shape = (N_ROW, N_COL, N_LAYER, TC)
    counts = jax.random.randint(count_key, grid_shape, TASKS // 4, TASKS + 1)
    top_place = jax.random.randint(top_key, (N_ROW, N_COL, N_LAYER, 1), 0, TC)
    half_place = (top_place + 1 + jax.random.randint(half_key, (N_ROW, N_COL, N_LAYER, 1), 0, TC - 1)) % TC
    tile_ids = jnp.arange(TC, dtype=jnp.int32)
    counts = jnp.where(tile_ids == half_place, TASKS // 2, counts)
    counts = jnp.where(tile_ids == top_place, TASKS, counts)
    entry_ids = jnp.arange(TASKS, dtype=jnp.int32)
    alive_mask = entry_ids < counts[..., None]
    return alive_mask.reshape(N_ROW, N_COL, N_LAYER, TC * TASKS)


def draw_a_slots(key, part):
    alive_mask = live_entries(key)
    key = jax.random.fold_in(key, 5)
    chosen = jax.random.randint(key, alive_mask.shape, 0, N_COL * TA)
    position = jnp.arange(TC * TASKS, dtype=jnp.int32)
    chosen = jnp.where(position == 0, 0, chosen)
    return jnp.where(alive_mask, chosen, N_COL * TA).astype(jnp.int32)


def draw_b_slots(key, part):
    alive_mask = live_entries(key)
    key = jax.random.fold_in(key, 9)
    chosen = jax.random.randint(key, alive_mask.shape, 0, N_ROW * TB)
    position = jnp.arange(TC * TASKS, dtype=jnp.int32)
    chosen = jnp.where(position == 0, N_ROW * TB - 1, chosen)
    return jnp.where(alive_mask, chosen, 0).astype(jnp.int32)


def level_of(key, extent, cuts, smallest, largest):
    gain, own = 1.0, jax.random.fold_in(key, 6)
    for dim, shards_of in cuts:
        heights = jnp.exp(jax.random.uniform(jax.random.fold_in(own, dim), (shards_of,), jnp.float32, smallest / len(cuts), largest / len(cuts)))
        gain = gain * jnp.repeat(heights, extent[dim] // shards_of).reshape([-1 if axis == dim else 1 for axis in range(len(extent))])
    return gain


def noise(rng, dims, spread, most, cuts=(), kind=jnp.bfloat16):
    level = level_of(rng, dims, cuts, -0.22, 0.18) if cuts else 1.0
    entries = jax.random.normal(rng, dims, jnp.float32) * spread * level
    return jnp.minimum(jnp.maximum(entries, -most), most).astype(kind)


def setup_inputs(seed: int = 0) -> dict:
    streams_of = jax.random.split(jax.random.key(seed), 5)
    return {
        "a_tiles": noise(streams_of[0], (N_ROW, N_LAYER, N_COL, TA, TILE * TILE), 1.0, 6.0, ((0, 4), (1, 4), (2, 16))),
        "b_tiles": noise(streams_of[1], (N_LAYER, N_ROW, N_COL, TB, TILE * TILE), (TASKS * TILE) ** -0.5, 0.25, ((0, 4), (1, 4), (2, 16))),
        "a_slots": draw_a_slots(jax.random.fold_in(streams_of[4], 71), 0),
        "b_slots": draw_b_slots(jax.random.fold_in(streams_of[4], 71), 0),
    }


def tile_sums(a_panel, b_panel, a_index, b_index):
    a_stack = a_panel[a_index].reshape(TC, TASKS, TILE, TILE).astype(jnp.float32)
    b_stack = b_panel[b_index].reshape(TC, TASKS, TILE, TILE).astype(jnp.float32)
    return jnp.einsum("sgik,sgkj->sij", a_stack, b_stack)


def reference(a_tiles, b_tiles, a_slots, b_slots):
    a_panels = a_tiles.reshape(N_ROW, N_LAYER, N_COL * TA, TILE, TILE)
    zero_tiles = jnp.zeros((N_ROW, N_LAYER, 1, TILE, TILE), a_tiles.dtype)
    a_panels = jnp.concatenate([a_panels, zero_tiles], axis=2)
    b_square = b_tiles.reshape(N_LAYER, N_ROW, N_COL, TB, TILE, TILE)
    b_panels = jnp.transpose(b_square, (0, 2, 1, 3, 4, 5)).reshape(N_LAYER, N_COL, N_ROW * TB, TILE, TILE)

    def one_panel(panel_id):
        grid_row = panel_id // N_COL
        grid_col = panel_id % N_COL
        running = jnp.zeros((TC, TILE, TILE), jnp.float32)
        for layer_part in range(N_LAYER):
            partial_value = tile_sums(a_panels[grid_row, layer_part], b_panels[layer_part, grid_col],
                                a_slots[grid_row, grid_col, layer_part], b_slots[grid_row, grid_col, layer_part])
            rounded = lax.optimization_barrier(partial_value.astype(jnp.bfloat16))
            running = running + rounded.astype(jnp.float32)
        return running.astype(jnp.bfloat16)

    c_all = lax.map(one_panel, jnp.arange(N_ROW * N_COL, dtype=jnp.int32))
    return c_all.reshape(N_ROW, N_COL, TC, TILE * TILE)
```

```python
import functools

import jax
import jax.numpy as jnp
from jax import lax
from jax.experimental import pallas as pl
from jax.experimental.pallas import tpu as pltpu
from jax.sharding import PartitionSpec as P

MESH = pl.DeviceIdType.MESH
TILE = 64
TASKS = 8
LANES = 128
PACK = TILE * TILE // LANES
TA = 8
TB = 16
HALF_A = 4
B_CHUNK = 4
OWNED = 24
CHUNK = 6
N_CHUNK = OWNED // CHUNK


def low_half(rows):
    return lax.broadcasted_iota(jnp.int32, (rows, LANES), 1) < TILE


def kernel(
    a_hbm, b_hbm, ai_hbm, bi_hbm, out_ref,
    a_raw, b_raw, ai, bi, a_wide, b_wide, b_mix, panel_a, panel_b, a_dup, b_dup,
    own_z, own_out, to_peer, from_peer, to_z, from_z, out_wide,
    in_sem, send_a, recv_a, send_b, recv_b, send_p, recv_p, send_z, recv_z,
):
    row = lax.axis_index("row")
    col = lax.axis_index("col")
    layer = lax.axis_index("layer")
    cx, cy = col // 4, col % 4
    zl, core = layer // 2, layer % 2

    def at_x(d):
        return (cx + d) % 4 * 4 + cy

    def at_y(d):
        return cx * 4 + (cy + d) % 4

    def dev(r=row, c=col, l=layer):
        return (r, c, l)

    peer = dev(l=zl * 2 + (1 - core))
    partner = dev(l=(1 - zl) * 2 + core)
    up, down = (row + 1) % 4, (row + 3) % 4

    copies = [
        pltpu.make_async_copy(b_hbm, b_raw, in_sem.at[0]),
        pltpu.make_async_copy(a_hbm, a_raw, in_sem.at[1]),
        pltpu.make_async_copy(ai_hbm, ai, in_sem.at[2]),
        pltpu.make_async_copy(bi_hbm, bi, in_sem.at[3]),
    ]
    for cp in copies:
        cp.start()

    barrier = pltpu.get_barrier_semaphore()
    others = [dev(c=at_x(d)) for d in (1, 2, 3)] + [dev(c=at_y(d)) for d in (1, 2, 3)]
    others += [dev(r=up), dev(r=down), peer, partner]
    for other in others:
        pl.semaphore_signal(barrier, inc=1, device_id=other, device_id_type=MESH)

    copies[0].wait()
    for j in range(PACK):
        b_wide[pl.ds(j * TB, TB)] = b_raw[:, j * LANES:(j + 1) * LANES].astype(jnp.float32)
    low16 = low_half(16)
    for t in range(TB):
        p0 = b_wide[pl.ds(t, 16, stride=TB)]
        p1 = b_wide[pl.ds(16 * TB + t, 16, stride=TB)]
        b_mix[pl.ds(t * PACK, 16, stride=2)] = jnp.where(low16, p0, pltpu.roll(p1, TILE, 1))
        b_mix[pl.ds(t * PACK + 1, 16, stride=2)] = jnp.where(low16, pltpu.roll(p0, TILE, 1), p1)
    for t in range(TB):
        panel_b[row * TB + t] = b_mix[pl.ds(t * PACK, PACK)].astype(jnp.bfloat16)
    copies[1].wait()
    for j in range(PACK):
        a_wide[pl.ds(j * TA, TA)] = a_raw[:, j * LANES:(j + 1) * LANES].astype(jnp.float32)
    for t in range(TA):
        panel_a[col * TA + t] = a_wide[pl.ds(t, PACK, stride=TA)].astype(jnp.bfloat16)

    pl.semaphore_wait(barrier, len(others))

    started = []

    def send(src, dst, ssem, rsem, device):
        cp = pltpu.make_async_remote_copy(
            src, dst, ssem, rsem, device_id=device, device_id_type=MESH
        )
        cp.start()
        started.append(cp)

    def b_part(h, c):
        return panel_b.at[pl.ds(h * TB + c * B_CHUNK, B_CHUNK)]

    def send_b_part(slot, h, c, device):
        send(b_part(h, c), b_part(h, c), send_b.at[slot], recv_b.at[h, c], device)

    def wait_b(h, c):
        pltpu.make_async_copy(b_part(h, c), b_part(h, c), recv_b.at[h, c]).wait()

    def a_part(half, g):
        return panel_a.at[pl.ds(g * TA + half * HALF_A, HALF_A)]

    def send_a_part(slot, half, g, device):
        send(a_part(half, g), a_part(half, g), send_a.at[slot], recv_a.at[half, g], device)

    def wait_a(half, g):
        pltpu.make_async_copy(a_part(half, g), a_part(half, g), recv_a.at[half, g]).wait()

    for i, c in enumerate((0, 1, 2, 3)):
        send_b_part(2 * i, row, c, dev(r=up))
        send_b_part(2 * i + 1, row, 3 - c, dev(r=down))
    slot = 0
    for d in (1, 3, 2):
        send_a_part(slot, 0, col, dev(c=at_x(d)))
        send_a_part(slot + 1, 1, col, dev(c=at_y(d)))
        slot += 2
    for d in (1, 3, 2):
        send_a_part(slot, 0, col, dev(c=at_y(d)))
        send_a_part(slot + 1, 1, col, dev(c=at_x(d)))
        slot += 2

    low32 = low_half(PACK)

    def spread_b(h, c):
        for i in range(B_CHUNK):
            t = h * TB + c * B_CHUNK + i
            q = panel_b[t]
            turned = pltpu.roll(q, TILE, 1)
            b_dup[t, 0:PACK] = jnp.where(low32, q, turned)
            b_dup[t, PACK:TILE] = jnp.where(low32, turned, q)

    def spread_a(half, g):
        for i in range(HALF_A):
            t = g * TA + half * HALF_A + i
            q = panel_a[t]
            turned = pltpu.roll(q, TILE, 1)
            a_dup[t, 0:PACK] = jnp.where(low32, q, turned)
            a_dup[t, PACK:TILE] = jnp.where(low32, turned, q)

    a_dup[16 * TA] = jnp.zeros((TILE, LANES), jnp.bfloat16)
    for half in range(2):
        spread_a(half, col)
    for c in range(4):
        spread_b(row, c)

    for d in (1, 3, 2):
        wait_a(0, at_x(d))
        for e in (1, 3, 2):
            send_a_part(slot, 0, at_x(d), dev(c=at_y(e)))
            slot += 1
        wait_a(1, at_y(d))
        for e in (1, 3, 2):
            send_a_part(slot, 1, at_y(d), dev(c=at_x(e)))
            slot += 1
        if d == 3:
            wait_b(down, 0)
            send_b_part(8, down, 0, dev(r=up))
            wait_b(up, 3)
            send_b_part(9, up, 3, dev(r=down))
    wait_b(down, 1)
    send_b_part(10, down, 1, dev(r=up))
    wait_b(up, 2)
    send_b_part(11, up, 2, dev(r=down))

    for d in (1, 3, 2):
        spread_a(0, at_x(d))
        spread_a(1, at_y(d))
    for c in (0, 1):
        spread_b(down, c)
        spread_b(up, 3 - c)
    for d in (1, 3, 2):
        for e in (0, 1, 3, 2):
            g = (cx + e) % 4 * 4 + (cy + d) % 4
            wait_a(0, g)
            spread_a(0, g)
            g = (cx + d) % 4 * 4 + (cy + e) % 4
            wait_a(1, g)
            spread_a(1, g)
    for c in (2, 3):
        wait_b(down, c)
        spread_b(down, c)
        wait_b(up, 3 - c)
        spread_b(up, 3 - c)
    far = (row + 2) % 4
    for c in (0, 3, 1, 2):
        wait_b(far, c)
        spread_b(far, c)

    copies[2].wait()
    copies[3].wait()
    low64 = low_half(TILE)

    def product(s):
        left = [
            jnp.where(low64, a_dup[ai[0, s * TASKS + 2 * p]], a_dup[ai[0, s * TASKS + 2 * p + 1]])
            for p in range(TASKS // 2)
        ]
        right = [b_dup[bi[0, s * TASKS + e]] for e in range(TASKS)]
        full = jnp.dot(
            jnp.concatenate(left, axis=1),
            jnp.concatenate(right, axis=0),
            preferred_element_type=jnp.float32,
        )
        return jnp.where(low32, full[:PACK], full[PACK:])

    g1 = ((1 - zl) * 2 + (1 - core)) * OWNED
    g2 = ((1 - zl) * 2 + core) * OWNED
    g3 = (zl * 2 + (1 - core)) * OWNED
    g4 = (zl * 2 + core) * OWNED

    def peer_copy(i):
        return pltpu.make_async_remote_copy(
            to_peer.at[pl.ds(i * CHUNK, CHUNK)], from_peer.at[pl.ds(i * CHUNK, CHUNK)],
            send_p.at[i], recv_p.at[i], device_id=peer, device_id_type=MESH,
        )

    def z_copy(i):
        return pltpu.make_async_remote_copy(
            to_z.at[pl.ds(i * CHUNK, CHUNK)], from_z.at[pl.ds(i * CHUNK, CHUNK)],
            send_z.at[i], recv_z.at[i], device_id=partner, device_id_type=MESH,
        )

    def for_peer(i, base):
        for k in range(CHUNK):
            to_peer[i * CHUNK + k] = product(base + (i % N_CHUNK) * CHUNK + k).astype(jnp.bfloat16)
        peer_copy(i).start()

    def send_on(i):
        peer_copy(i).wait_recv()
        for k in range(CHUNK):
            s = i * CHUNK + k
            to_z[s] = (own_z[s] + from_peer[s].astype(jnp.float32)).astype(jnp.bfloat16)
        z_copy(i).start()

    def first(i, carry):
        for_peer(i, g1)
        for k in range(CHUNK):
            own_z[i * CHUNK + k] = product(g2 + i * CHUNK + k)

        @pl.when(i > 0)
        def _():
            send_on(i - 1)
        return carry

    lax.fori_loop(0, N_CHUNK, first, 0)

    def second(i, carry):
        for_peer(N_CHUNK + i, g3)

        @pl.when(i == 0)
        def _():
            send_on(N_CHUNK - 1)
        for k in range(CHUNK):
            own_out[i * CHUNK + k] = product(g4 + i * CHUNK + k)
        return carry

    lax.fori_loop(0, N_CHUNK, second, 0)

    def third(i, carry):
        peer_copy(N_CHUNK + i).wait_recv()
        z_copy(i).wait_recv()
        for k in range(CHUNK):
            s = i * CHUNK + k
            total = own_out[s] + from_peer[OWNED + s].astype(jnp.float32) + from_z[s].astype(jnp.float32)
            out_wide[pl.ds(s, PACK, stride=OWNED)] = total
        return carry

    lax.fori_loop(0, N_CHUNK, third, 0)
    for j in range(PACK):
        out_ref[:, j * LANES:(j + 1) * LANES] = out_wide[pl.ds(j * OWNED, OWNED)].astype(jnp.bfloat16)

    for cp in started:
        cp.wait_send()
    for i in range(2 * N_CHUNK):
        peer_copy(i).wait_send()
    for i in range(N_CHUNK):
        z_copy(i).wait_send()


def shards(a_tiles, b_tiles, a_slots, b_slots):
    flat = TILE * TILE
    bf16, f32 = jnp.bfloat16, jnp.float32
    out = pl.pallas_call(
        kernel,
        out_shape=jax.ShapeDtypeStruct((OWNED, flat), bf16),
        in_specs=[pl.BlockSpec(memory_space=pl.ANY)] * 4,
        out_specs=pl.BlockSpec(memory_space=pltpu.VMEM),
        scratch_shapes=[
            pltpu.VMEM((TA, flat), bf16),
            pltpu.VMEM((TB, flat), bf16),
            pltpu.SMEM((1, 768), jnp.int32),
            pltpu.SMEM((1, 768), jnp.int32),
            pltpu.VMEM((TA * PACK, LANES), f32),
            pltpu.VMEM((TB * PACK, LANES), f32),
            pltpu.VMEM((TB * PACK, LANES), f32),
            pltpu.VMEM((16 * TA, PACK, LANES), bf16),
            pltpu.VMEM((4 * TB, PACK, LANES), bf16),
            pltpu.VMEM((16 * TA + 1, TILE, LANES), bf16),
            pltpu.VMEM((4 * TB, TILE, LANES), bf16),
            pltpu.VMEM((OWNED, PACK, LANES), f32),
            pltpu.VMEM((OWNED, PACK, LANES), f32),
            pltpu.VMEM((2 * OWNED, PACK, LANES), bf16),
            pltpu.VMEM((2 * OWNED, PACK, LANES), bf16),
            pltpu.VMEM((OWNED, PACK, LANES), bf16),
            pltpu.VMEM((OWNED, PACK, LANES), bf16),
            pltpu.VMEM((PACK * OWNED, LANES), f32),
            pltpu.SemaphoreType.DMA((4,)),
            pltpu.SemaphoreType.DMA((30,)),
            pltpu.SemaphoreType.DMA((2, 16)),
            pltpu.SemaphoreType.DMA((12,)),
            pltpu.SemaphoreType.DMA((4, 4)),
            pltpu.SemaphoreType.DMA((2 * N_CHUNK,)),
            pltpu.SemaphoreType.DMA((2 * N_CHUNK,)),
            pltpu.SemaphoreType.DMA((N_CHUNK,)),
            pltpu.SemaphoreType.DMA((N_CHUNK,)),
        ],
        compiler_params=pltpu.CompilerParams(
            collective_id=0, has_side_effects=True, vmem_limit_bytes=60 * 2**20
        ),
        name="purify",
    )(
        a_tiles.reshape(TA, flat), b_tiles.reshape(TB, flat),
        a_slots.reshape(1, -1), b_slots.reshape(1, -1),
    )
    return out.reshape(1, 1, OWNED, flat)


def solution(mesh):
    in_specs = (
        P("row", "layer", "col", None, None),
        P("layer", "row", "col", None, None),
        P("row", "col", "layer", None),
        P("row", "col", "layer", None),
    )
    out_specs = P("row", "col", "layer", None)
    return jax.shard_map(shards, mesh=mesh, in_specs=in_specs, out_specs=out_specs, check_vma=False)
```

```python
import jax
import jax.numpy as jnp
from jax import lax
from jax.experimental import pallas as pl
from jax.experimental.pallas import tpu as pltpu
from jax.sharding import PartitionSpec as P

MESH = pl.DeviceIdType.MESH
TILE = 64
TASKS = 8
LANES = 128
PACK = TILE * TILE // LANES
TA = 8
TB = 16
A_COLS = 2048
B_COLS = 1024
OWNED = 24
Z_CUTS = ((0, 4), (4, 6), (10, 8), (18, 6))
PEER_CUTS = Z_CUTS + ((24, 12), (36, 12))


def low_half(rows):
    return lax.broadcasted_iota(jnp.int32, (rows, LANES), 1) < TILE


def kernel(
    a_hbm, b_hbm, ai_hbm, bi_hbm, out_ref,
    a_raw, b_raw, ai, bi, a_wide, b_wide, b_mix, panel_a, panel_b, a_dup, b_dup,
    own_z, own_out, to_peer, from_peer, to_z, from_z, out_wide,
    in_sem, send_a, recv_a, send_b, recv_b, send_p, recv_p, send_z, recv_z,
):
    row = lax.axis_index("row")
    col = lax.axis_index("col")
    layer = lax.axis_index("layer")
    cx, cy = col // 4, col % 4
    zl, core = layer // 2, layer % 2

    def at_x(d):
        return (cx + d) % 4 * 4 + cy

    def at_y(d):
        return cx * 4 + (cy + d) % 4

    def dev(r=row, c=col, l=layer):
        return (r, c, l)

    peer = dev(l=zl * 2 + (1 - core))
    partner = dev(l=(1 - zl) * 2 + core)
    up, down = (row + 1) % 4, (row + 3) % 4
    far = (row + 2) % 4

    barrier = pltpu.get_barrier_semaphore()
    others = [dev(c=at_x(d)) for d in (1, 2, 3)] + [dev(c=at_y(d)) for d in (1, 2, 3)]
    others += [dev(r=up), dev(r=down), peer, partner]
    for other in others:
        pl.semaphore_signal(barrier, inc=1, device_id=other, device_id_type=MESH)

    def b_in(c):
        cut = pl.ds(c * B_COLS, B_COLS)
        return pltpu.make_async_copy(b_hbm.at[:, cut], b_raw.at[:, cut], in_sem.at[c])

    def a_in(half):
        cut = pl.ds(half * A_COLS, A_COLS)
        return pltpu.make_async_copy(a_hbm.at[:, cut], a_raw.at[:, cut], in_sem.at[4 + half])

    ai_in = pltpu.make_async_copy(ai_hbm, ai, in_sem.at[6])
    bi_in = pltpu.make_async_copy(bi_hbm, bi, in_sem.at[7])
    for cp in (b_in(0), b_in(3), a_in(0), a_in(1), b_in(1), b_in(2), ai_in, bi_in):
        cp.start()

    low8, low16, low32, low64 = (low_half(n) for n in (8, 16, 32, 64))

    def pack_b(c):
        b_in(c).wait()
        for j in range(8 * c, 8 * c + 8):
            b_wide[pl.ds(j * TB, TB)] = b_raw[:, j * LANES:(j + 1) * LANES].astype(jnp.float32)
        for u in range(8):
            p = b_wide[pl.ds(8 * c * TB + u, 8, stride=TB)]
            q = b_wide[pl.ds(8 * c * TB + u + 8, 8, stride=TB)]
            base = (c * 8 + u) * 16
            b_mix[pl.ds(base, 8, stride=2)] = jnp.where(low8, p, pltpu.roll(q, TILE, 1))
            b_mix[pl.ds(base + 1, 8, stride=2)] = jnp.where(low8, pltpu.roll(p, TILE, 1), q)
        for u in range(8):
            panel_b[row, c, u] = b_mix[pl.ds((c * 8 + u) * 16, 16)].astype(jnp.bfloat16)

    def pack_a(half):
        a_in(half).wait()
        for j in range(16 * half, 16 * half + 16):
            a_wide[pl.ds(j * TA, TA)] = a_raw[:, j * LANES:(j + 1) * LANES].astype(jnp.float32)
        for t in range(TA):
            panel_a[half, col, t] = a_wide[pl.ds(half * 16 * TA + t, 16, stride=TA)].astype(jnp.bfloat16)

    started = []

    def send(src, dst, ssem, rsem, device):
        cp = pltpu.make_async_remote_copy(
            src, dst, ssem, rsem, device_id=device, device_id_type=MESH
        )
        cp.start()
        started.append(cp)

    b_sent, a_sent = [], []

    def send_b_part(h, c, device):
        part = panel_b.at[h, c]
        send(part, part, send_b.at[len(b_sent)], recv_b.at[h, c], device)
        b_sent.append(c)

    def wait_b(h, c):
        part = panel_b.at[h, c]
        pltpu.make_async_copy(part, part, recv_b.at[h, c]).wait()

    def send_a_part(half, g, device):
        part = panel_a.at[half, g]
        send(part, part, send_a.at[len(a_sent)], recv_a.at[half, g], device)
        a_sent.append(half)

    def wait_a(half, g):
        part = panel_a.at[half, g]
        pltpu.make_async_copy(part, part, recv_a.at[half, g]).wait()

    def along_x(half, g):
        for d in (1, 3, 2):
            send_a_part(half, g, dev(c=at_x(d)))

    def along_y(half, g):
        for d in (1, 3, 2):
            send_a_part(half, g, dev(c=at_y(d)))

    def spread_b(h, c):
        rows = pl.ds(16 * c, 16)
        for u in range(8):
            q = panel_b[h, c, u]
            turned = pltpu.roll(q, TILE, 1)
            b_dup[h * TB + u, rows] = jnp.where(low16, q, turned)
            b_dup[h * TB + 8 + u, rows] = jnp.where(low16, turned, q)

    def spread_a(half, g):
        for t in range(TA):
            q = panel_a[half, g, t]
            turned = pltpu.roll(q, TILE, 1)
            a_dup[g * TA + t, pl.ds(16 * half, 16)] = jnp.where(low16, q, turned)
            a_dup[g * TA + t, pl.ds(32 + 16 * half, 16)] = jnp.where(low16, turned, q)

    pack_b(0)
    pack_b(3)
    pl.semaphore_wait(barrier, len(others))
    send_b_part(row, 0, dev(r=up))
    send_b_part(row, 3, dev(r=down))
    pack_a(0)
    along_x(0, col)
    pack_a(1)
    along_y(1, col)
    pack_b(1)
    send_b_part(row, 1, dev(r=up))
    pack_b(2)
    send_b_part(row, 2, dev(r=down))
    along_y(0, col)
    along_x(1, col)
    for c in (2, 3):
        send_b_part(row, c, dev(r=up))
        send_b_part(row, 3 - c, dev(r=down))

    a_dup[16 * TA] = jnp.zeros((TILE, LANES), jnp.bfloat16)
    for half in range(2):
        spread_a(half, col)
    for c in range(4):
        spread_b(row, c)

    def pass_on_a(d):
        wait_a(0, at_x(d))
        along_y(0, at_x(d))
        wait_a(1, at_y(d))
        along_x(1, at_y(d))

    def pass_on_b(c):
        wait_b(down, c)
        send_b_part(down, c, dev(r=up))
        wait_b(up, 3 - c)
        send_b_part(up, 3 - c, dev(r=down))

    pass_on_a(1)
    pass_on_a(3)
    pass_on_b(0)
    pass_on_a(2)
    pass_on_b(1)

    for d in (1, 3, 2):
        spread_a(0, at_x(d))
        spread_a(1, at_y(d))
    for c in (0, 1):
        spread_b(down, c)
        spread_b(up, 3 - c)
    for d in (1, 3, 2):
        for e in (0, 1, 3, 2):
            g = (cx + e) % 4 * 4 + (cy + d) % 4
            wait_a(0, g)
            spread_a(0, g)
            g = (cx + d) % 4 * 4 + (cy + e) % 4
            wait_a(1, g)
            spread_a(1, g)
    for c in (2, 3):
        wait_b(down, c)
        spread_b(down, c)
        wait_b(up, 3 - c)
        spread_b(up, 3 - c)
    for c in (0, 3, 1, 2):
        wait_b(far, c)
        spread_b(far, c)
    ai_in.wait()
    bi_in.wait()

    def product(s):
        left = [
            jnp.where(low64, a_dup[ai[0, s * TASKS + 2 * p]], a_dup[ai[0, s * TASKS + 2 * p + 1]])
            for p in range(TASKS // 2)
        ]
        right = [b_dup[bi[0, s * TASKS + e]] for e in range(TASKS)]
        full = jnp.dot(
            jnp.concatenate(left, axis=1),
            jnp.concatenate(right, axis=0),
            preferred_element_type=jnp.float32,
        )
        return jnp.where(low32, full[:PACK], full[PACK:])

    g1 = ((1 - zl) * 2 + (1 - core)) * OWNED
    g2 = ((1 - zl) * 2 + core) * OWNED
    g3 = (zl * 2 + (1 - core)) * OWNED
    g4 = (zl * 2 + core) * OWNED

    def peer_copy(i):
        first, count = PEER_CUTS[i]
        cut = pl.ds(first, count)
        return pltpu.make_async_remote_copy(
            to_peer.at[cut], from_peer.at[cut], send_p.at[i], recv_p.at[i],
            device_id=peer, device_id_type=MESH,
        )

    def z_copy(i):
        first, count = Z_CUTS[i]
        cut = pl.ds(first, count)
        return pltpu.make_async_remote_copy(
            to_z.at[cut], from_z.at[cut], send_z.at[i], recv_z.at[i],
            device_id=partner, device_id_type=MESH,
        )

    def for_peer(i, base):
        first, count = PEER_CUTS[i]
        for s in range(first, first + count):
            to_peer[s] = product(base + s % OWNED).astype(jnp.bfloat16)
        peer_copy(i).start()

    def for_z(i):
        first, count = Z_CUTS[i]
        for s in range(first, first + count):
            own_z[s] = product(g2 + s)

    def send_on(i):
        first, count = Z_CUTS[i]
        peer_copy(i).wait_recv()
        for s in range(first, first + count):
            to_z[s] = (own_z[s] + from_peer[s].astype(jnp.float32)).astype(jnp.bfloat16)
        z_copy(i).start()

    n_z, n_peer = len(Z_CUTS), len(PEER_CUTS)
    for_peer(0, g1)
    for_z(0)
    for_peer(1, g1)
    for_z(1)
    for_peer(2, g1)
    for_z(2)
    send_on(0)
    send_on(1)
    for_peer(3, g1)
    for_z(3)
    send_on(2)
    send_on(3)
    for i in range(n_z, n_peer):
        for_peer(i, g3)
    for s in range(OWNED):
        own_out[s] = product(g4 + s)
    for i in range(n_z, n_peer):
        peer_copy(i).wait_recv()
        first, count = PEER_CUTS[i]
        for s in range(first, first + count):
            own_out[s - OWNED] += from_peer[s].astype(jnp.float32)
    for i in range(n_z):
        first, count = Z_CUTS[i]
        z_copy(i).wait_recv()
        for s in range(first, first + count):
            out_wide[pl.ds(s, PACK, stride=OWNED)] = own_out[s] + from_z[s].astype(jnp.float32)
    for j in range(PACK):
        out_ref[:, j * LANES:(j + 1) * LANES] = out_wide[pl.ds(j * OWNED, OWNED)].astype(jnp.bfloat16)

    for cp in started:
        cp.wait_send()
    for i in range(n_peer):
        peer_copy(i).wait_send()
    for i in range(n_z):
        z_copy(i).wait_send()


def shards(a_tiles, b_tiles, a_slots, b_slots):
    flat = TILE * TILE
    bf16, f32 = jnp.bfloat16, jnp.float32
    out = pl.pallas_call(
        kernel,
        out_shape=pltpu.VMEM((OWNED, flat), bf16),
        in_specs=[pl.BlockSpec(memory_space=pl.ANY)] * 4,
        out_specs=pl.BlockSpec(memory_space=pltpu.VMEM),
        scratch_shapes=[
            pltpu.VMEM((TA, flat), bf16),
            pltpu.VMEM((TB, flat), bf16),
            pltpu.SMEM((1, 768), jnp.int32),
            pltpu.SMEM((1, 768), jnp.int32),
            pltpu.VMEM((TA * PACK, LANES), f32),
            pltpu.VMEM((TB * PACK, LANES), f32),
            pltpu.VMEM((TB * PACK, LANES), f32),
            pltpu.VMEM((2, 16, TA, 16, LANES), bf16),
            pltpu.VMEM((4, 4, TB // 2, 16, LANES), bf16),
            pltpu.VMEM((16 * TA + 1, TILE, LANES), bf16),
            pltpu.VMEM((4 * TB, TILE, LANES), bf16),
            pltpu.VMEM((OWNED, PACK, LANES), f32),
            pltpu.VMEM((OWNED, PACK, LANES), f32),
            pltpu.VMEM((2 * OWNED, PACK, LANES), bf16),
            pltpu.VMEM((2 * OWNED, PACK, LANES), bf16),
            pltpu.VMEM((OWNED, PACK, LANES), bf16),
            pltpu.VMEM((OWNED, PACK, LANES), bf16),
            pltpu.VMEM((PACK * OWNED, LANES), f32),
            pltpu.SemaphoreType.DMA((8,)),
            pltpu.SemaphoreType.DMA((30,)),
            pltpu.SemaphoreType.DMA((2, 16)),
            pltpu.SemaphoreType.DMA((12,)),
            pltpu.SemaphoreType.DMA((4, 4)),
            pltpu.SemaphoreType.DMA((len(PEER_CUTS),)),
            pltpu.SemaphoreType.DMA((len(PEER_CUTS),)),
            pltpu.SemaphoreType.DMA((len(Z_CUTS),)),
            pltpu.SemaphoreType.DMA((len(Z_CUTS),)),
        ],
        compiler_params=pltpu.CompilerParams(
            collective_id=0, has_side_effects=True, vmem_limit_bytes=60 * 2**20
        ),
        name="purify",
    )(
        a_tiles.reshape(TA, flat), b_tiles.reshape(TB, flat),
        a_slots.reshape(1, -1), b_slots.reshape(1, -1),
    )
    return out.reshape(1, 1, OWNED, flat)


def solution(mesh):
    in_specs = (
        P("row", "layer", "col", None, None),
        P("layer", "row", "col", None, None),
        P("row", "col", "layer", None),
        P("row", "col", "layer", None),
    )
    out_specs = P("row", "col", "layer", None)
    return jax.shard_map(shards, mesh=mesh, in_specs=in_specs, out_specs=out_specs, check_vma=False)
```

```python
import jax
import jax.numpy as jnp
from jax import lax
from jax.experimental import pallas as pl
from jax.experimental.pallas import tpu as pltpu
from jax.sharding import PartitionSpec as P

MESH = pl.DeviceIdType.MESH
TILE = 64
TASKS = 8
LANES = 128
PACK = TILE * TILE // LANES
TA = 8
TB = 16
A_COLS = 2048
B_COLS = 1024
OWNED = 24
N_SEND_A = 30
HIGH_BY_CROSS = (0, 1, 2)
LOW_BY_CROSS = (0, 1, 2)
N_LOW_B = 12 + len(HIGH_BY_CROSS) - len(LOW_BY_CROSS)
N_HIGH_B = 12 + len(LOW_BY_CROSS) - len(HIGH_BY_CROSS)
Z_CUTS = ((0, 4), (4, 6), (10, 8), (18, 6))
PEER_CUTS = Z_CUTS + ((24, 12), (36, 12))


def low_half(rows):
    return lax.broadcasted_iota(jnp.int32, (rows, LANES), 1) < TILE


def kernel(
    a_hbm, b_hbm, ai_hbm, bi_hbm, out_ref,
    a_raw, b_raw, ai, bi, a_wide, b_wide, b_mix, panel_a, panel_b, a_dup, b_dup,
    own_z, own_out, to_peer, from_peer, to_z, from_z, out_wide,
    in_sem, ready, send_a, recv_a, send_b, recv_b, send_p, recv_p, send_z, recv_z,
):
    row = lax.axis_index("row")
    col = lax.axis_index("col")
    layer = lax.axis_index("layer")
    cx, cy = col // 4, col % 4
    zl, core = layer // 2, layer % 2

    def at_x(d):
        return (cx + d) % 4 * 4 + cy

    def at_y(d):
        return cx * 4 + (cy + d) % 4

    def dev(r=row, c=col, l=layer):
        return (r, c, l)

    peer = dev(l=zl * 2 + (1 - core))
    partner = dev(l=(1 - zl) * 2 + core)
    mate, cross, far = row + 1 - 2 * (row % 2), 3 - row, (row + 2) % 4
    is_low = row < 2

    barrier = pltpu.get_barrier_semaphore()

    @pl.when(is_low)
    def _():
        pl.semaphore_signal(barrier, inc=1, device_id=dev(r=cross), device_id_type=MESH)

    friends = [dev(r=mate)] + [dev(c=at(d)) for d in (2, 1, 3) for at in (at_x, at_y)] + [partner, peer]
    for other in friends:
        pl.semaphore_signal(barrier, inc=1, device_id=other, device_id_type=MESH)

    def b_in(c):
        cut = pl.ds(c * B_COLS, B_COLS)
        return pltpu.make_async_copy(b_hbm.at[:, cut], b_raw.at[:, cut], in_sem.at[c])

    def a_in(half):
        cut = pl.ds(half * A_COLS, A_COLS)
        return pltpu.make_async_copy(a_hbm.at[:, cut], a_raw.at[:, cut], in_sem.at[4 + half])

    ai_in = pltpu.make_async_copy(ai_hbm, ai, in_sem.at[6])
    bi_in = pltpu.make_async_copy(bi_hbm, bi, in_sem.at[7])
    for cp in (b_in(0), b_in(3), a_in(0), a_in(1), b_in(1), b_in(2), ai_in, bi_in):
        cp.start()

    low8, low16, low32, low64 = (low_half(n) for n in (8, 16, 32, 64))

    def pack_b(c):
        b_in(c).wait()
        for j in range(8 * c, 8 * c + 8):
            b_wide[pl.ds(j * TB, TB)] = b_raw[:, j * LANES:(j + 1) * LANES].astype(jnp.float32)
        for u in range(8):
            p = b_wide[pl.ds(8 * c * TB + u, 8, stride=TB)]
            q = b_wide[pl.ds(8 * c * TB + u + 8, 8, stride=TB)]
            base = (c * 8 + u) * 16
            b_mix[pl.ds(base, 8, stride=2)] = jnp.where(low8, p, pltpu.roll(q, TILE, 1))
            b_mix[pl.ds(base + 1, 8, stride=2)] = jnp.where(low8, pltpu.roll(p, TILE, 1), q)
        for u in range(8):
            panel_b[row, c, u] = b_mix[pl.ds((c * 8 + u) * 16, 16)].astype(jnp.bfloat16)

    def pack_a(half):
        a_in(half).wait()
        for j in range(16 * half, 16 * half + 16):
            a_wide[pl.ds(j * TA, TA)] = a_raw[:, j * LANES:(j + 1) * LANES].astype(jnp.float32)
        for t in range(TA):
            panel_a[half, col, t] = a_wide[pl.ds(half * 16 * TA + t, 16, stride=TA)].astype(jnp.bfloat16)

    def wait_b(h, c):
        part = panel_b.at[h, c]
        pltpu.make_async_copy(part, part, recv_b.at[h, c]).wait()

    def wait_a(half, g):
        part = panel_a.at[half, g]
        pltpu.make_async_copy(part, part, recv_a.at[half, g]).wait()

    def spread_b(h, c):
        rows = pl.ds(16 * c, 16)
        for u in range(8):
            q = panel_b[h, c, u]
            turned = pltpu.roll(q, TILE, 1)
            b_dup[h * TB + u, rows] = jnp.where(low16, q, turned)
            b_dup[h * TB + 8 + u, rows] = jnp.where(low16, turned, q)

    def spread_a(half, g):
        for t in range(TA):
            q = panel_a[half, g, t]
            turned = pltpu.roll(q, TILE, 1)
            a_dup[g * TA + t, pl.ds(16 * half, 16)] = jnp.where(low16, q, turned)
            a_dup[g * TA + t, pl.ds(32 + 16 * half, 16)] = jnp.where(low16, turned, q)

    def gather(low):
        count = {"a": 0, "b": 0}

        def send(kind, part, ssem, rsem, device):
            pltpu.make_async_remote_copy(
                part, part, ssem.at[count[kind]], rsem, device_id=device, device_id_type=MESH
            ).start()
            count[kind] += 1

        def b_to(r, h, c):
            send("b", panel_b.at[h, c], send_b, recv_b.at[h, c], dev(r=r))

        def along_x(half, g):
            for d in (1, 3, 2):
                send("a", panel_a.at[half, g], send_a, recv_a.at[half, g], dev(c=at_x(d)))

        def along_y(half, g):
            for d in (1, 3, 2):
                send("a", panel_a.at[half, g], send_a, recv_a.at[half, g], dev(c=at_y(d)))

        def pass_on_a(d):
            wait_a(0, at_x(d))
            along_y(0, at_x(d))
            wait_a(1, at_y(d))
            along_x(1, at_y(d))

        def pass_on_b(source, c, r):
            wait_b(source, c)
            b_to(r, source, c)

        def spread_own():
            a_dup[16 * TA] = jnp.zeros((TILE, LANES), jnp.bfloat16)
            for half in range(2):
                spread_a(half, col)
            for c in range(4):
                spread_b(row, c)

        if low:
            pack_a(0)
            pl.semaphore_wait(barrier, len(friends))
            along_x(0, col)
            pack_a(1)
            along_y(1, col)
            for c in (3, 2, 1, 0):
                pack_b(c)
                b_to(mate, row, c)
            along_y(0, col)
            along_x(1, col)
            spread_own()
            for d in (1, 3, 2):
                pass_on_a(d)
            pl.semaphore_wait(ready, 1)
            for c in range(4):
                b_to(cross, row, c)
                if c not in LOW_BY_CROSS:
                    pass_on_b(mate, c, cross)
            for c in HIGH_BY_CROSS:
                pass_on_b(cross, c, mate)
        else:
            pack_b(0)
            pl.semaphore_wait(barrier, len(friends) + 1)
            pl.semaphore_signal(ready, inc=1, device_id=dev(r=cross), device_id_type=MESH)
            b_to(cross, row, 0)
            pack_b(3)
            b_to(mate, row, 3)
            pack_b(1)
            b_to(cross, row, 1)
            pack_b(2)
            b_to(cross, row, 2)
            b_to(cross, row, 3)
            pack_a(0)
            along_x(0, col)
            pack_a(1)
            along_y(1, col)
            along_y(0, col)
            along_x(1, col)
            for c in (0, 1, 2):
                b_to(mate, row, c)
            spread_own()
            pass_on_a(1)
            pass_on_a(3)
            for c in range(4):
                if c not in HIGH_BY_CROSS:
                    pass_on_b(mate, c, cross)
            pass_on_a(2)
            for c in LOW_BY_CROSS:
                pass_on_b(cross, c, mate)

    @pl.when(is_low)
    def _():
        gather(True)

    @pl.when(jnp.logical_not(is_low))
    def _():
        gather(False)

    def later(low, source, c):
        passed = HIGH_BY_CROSS if low else LOW_BY_CROSS
        other = LOW_BY_CROSS if low else HIGH_BY_CROSS
        return c not in passed if source == "cross" else c in other

    def last_waits(low):
        for d in (1, 3, 2):
            spread_a(0, at_x(d))
            spread_a(1, at_y(d))

        def rest_of_a(d):
            for e in (0, 1, 3, 2):
                g = (cx + e) % 4 * 4 + (cy + d) % 4
                wait_a(0, g)
                spread_a(0, g)
                g = (cx + d) % 4 * 4 + (cy + e) % 4
                wait_a(1, g)
                spread_a(1, g)

        rest_of_a(1)
        for c in range(4):
            if later(low, "cross", c):
                wait_b(cross, c)
            spread_b(cross, c)
            if later(low, "mate", c):
                wait_b(mate, c)
            spread_b(mate, c)
        rest_of_a(3)
        rest_of_a(2)
        for c in range(4):
            wait_b(far, c)
            spread_b(far, c)

    @pl.when(is_low)
    def _():
        last_waits(True)

    @pl.when(jnp.logical_not(is_low))
    def _():
        last_waits(False)

    ai_in.wait()
    bi_in.wait()

    def product(s):
        left = [
            jnp.where(low64, a_dup[ai[0, s * TASKS + 2 * p]], a_dup[ai[0, s * TASKS + 2 * p + 1]])
            for p in range(TASKS // 2)
        ]
        right = [b_dup[bi[0, s * TASKS + e]] for e in range(TASKS)]
        full = jnp.dot(
            jnp.concatenate(left, axis=1),
            jnp.concatenate(right, axis=0),
            preferred_element_type=jnp.float32,
        )
        return jnp.where(low32, full[:PACK], full[PACK:])

    g1 = ((1 - zl) * 2 + (1 - core)) * OWNED
    g2 = ((1 - zl) * 2 + core) * OWNED
    g3 = (zl * 2 + (1 - core)) * OWNED
    g4 = (zl * 2 + core) * OWNED

    def peer_copy(i):
        first, count = PEER_CUTS[i]
        cut = pl.ds(first, count)
        return pltpu.make_async_remote_copy(
            to_peer.at[cut], from_peer.at[cut], send_p.at[i], recv_p.at[i],
            device_id=peer, device_id_type=MESH,
        )

    def z_copy(i):
        first, count = Z_CUTS[i]
        cut = pl.ds(first, count)
        return pltpu.make_async_remote_copy(
            to_z.at[cut], from_z.at[cut], send_z.at[i], recv_z.at[i],
            device_id=partner, device_id_type=MESH,
        )

    def for_peer(i, base):
        first, count = PEER_CUTS[i]
        for s in range(first, first + count):
            to_peer[s] = product(base + s % OWNED).astype(jnp.bfloat16)
        peer_copy(i).start()

    def for_z(i):
        first, count = Z_CUTS[i]
        for s in range(first, first + count):
            own_z[s] = product(g2 + s)

    def send_on(i):
        first, count = Z_CUTS[i]
        peer_copy(i).wait_recv()
        for s in range(first, first + count):
            to_z[s] = (own_z[s] + from_peer[s].astype(jnp.float32)).astype(jnp.bfloat16)
        z_copy(i).start()

    n_z, n_peer = len(Z_CUTS), len(PEER_CUTS)
    for_peer(0, g1)
    for_z(0)
    for_peer(1, g1)
    for_z(1)
    for_peer(2, g1)
    for_z(2)
    send_on(0)
    send_on(1)
    for_peer(3, g1)
    for_z(3)
    send_on(2)
    send_on(3)
    for i in range(n_z, n_peer):
        for_peer(i, g3)
    for s in range(OWNED):
        own_out[s] = product(g4 + s)
    for i in range(n_z, n_peer):
        peer_copy(i).wait_recv()
        first, count = PEER_CUTS[i]
        for s in range(first, first + count):
            own_out[s - OWNED] += from_peer[s].astype(jnp.float32)
    for i in range(n_z):
        first, count = Z_CUTS[i]
        z_copy(i).wait_recv()
        for s in range(first, first + count):
            out_wide[pl.ds(s, PACK, stride=OWNED)] = own_out[s] + from_z[s].astype(jnp.float32)
    for j in range(PACK):
        out_ref[:, j * LANES:(j + 1) * LANES] = out_wide[pl.ds(j * OWNED, OWNED)].astype(jnp.bfloat16)

    for i in range(N_SEND_A):
        pltpu.make_async_copy(panel_a.at[0, 0], panel_a.at[0, 0], send_a.at[i]).wait()
    def b_sent(first, last):
        for i in range(first, last):
            pltpu.make_async_copy(panel_b.at[0, 0], panel_b.at[0, 0], send_b.at[i]).wait()

    @pl.when(is_low)
    def _():
        b_sent(0, N_LOW_B)

    @pl.when(jnp.logical_not(is_low))
    def _():
        b_sent(0, N_HIGH_B)

    for i in range(n_peer):
        peer_copy(i).wait_send()
    for i in range(n_z):
        z_copy(i).wait_send()


def shards(a_tiles, b_tiles, a_slots, b_slots):
    flat = TILE * TILE
    bf16, f32 = jnp.bfloat16, jnp.float32
    out = pl.pallas_call(
        kernel,
        out_shape=pltpu.VMEM((OWNED, flat), bf16),
        in_specs=[pl.BlockSpec(memory_space=pl.ANY)] * 4,
        out_specs=pl.BlockSpec(memory_space=pltpu.VMEM),
        scratch_shapes=[
            pltpu.VMEM((TA, flat), bf16),
            pltpu.VMEM((TB, flat), bf16),
            pltpu.SMEM((1, 768), jnp.int32),
            pltpu.SMEM((1, 768), jnp.int32),
            pltpu.VMEM((TA * PACK, LANES), f32),
            pltpu.VMEM((TB * PACK, LANES), f32),
            pltpu.VMEM((TB * PACK, LANES), f32),
            pltpu.VMEM((2, 16, TA, 16, LANES), bf16),
            pltpu.VMEM((4, 4, TB // 2, 16, LANES), bf16),
            pltpu.VMEM((16 * TA + 1, TILE, LANES), bf16),
            pltpu.VMEM((4 * TB, TILE, LANES), bf16),
            pltpu.VMEM((OWNED, PACK, LANES), f32),
            pltpu.VMEM((OWNED, PACK, LANES), f32),
            pltpu.VMEM((2 * OWNED, PACK, LANES), bf16),
            pltpu.VMEM((2 * OWNED, PACK, LANES), bf16),
            pltpu.VMEM((OWNED, PACK, LANES), bf16),
            pltpu.VMEM((OWNED, PACK, LANES), bf16),
            pltpu.VMEM((PACK * OWNED, LANES), f32),
            pltpu.SemaphoreType.DMA((8,)),
            pltpu.SemaphoreType.REGULAR,
            pltpu.SemaphoreType.DMA((N_SEND_A,)),
            pltpu.SemaphoreType.DMA((2, 16)),
            pltpu.SemaphoreType.DMA((16,)),
            pltpu.SemaphoreType.DMA((4, 4)),
            pltpu.SemaphoreType.DMA((len(PEER_CUTS),)),
            pltpu.SemaphoreType.DMA((len(PEER_CUTS),)),
            pltpu.SemaphoreType.DMA((len(Z_CUTS),)),
            pltpu.SemaphoreType.DMA((len(Z_CUTS),)),
        ],
        compiler_params=pltpu.CompilerParams(
            collective_id=0, has_side_effects=True, vmem_limit_bytes=60 * 2**20
        ),
        name="purify",
    )(
        a_tiles.reshape(TA, flat), b_tiles.reshape(TB, flat),
        a_slots.reshape(1, -1), b_slots.reshape(1, -1),
    )
    return out.reshape(1, 1, OWNED, flat)


def solution(mesh):
    in_specs = (
        P("row", "layer", "col", None, None),
        P("layer", "row", "col", None, None),
        P("row", "col", "layer", None),
        P("row", "col", "layer", None),
    )
    out_specs = P("row", "col", "layer", None)
    return jax.shard_map(shards, mesh=mesh, in_specs=in_specs, out_specs=out_specs, check_vma=False)
```

```python
import jax
import jax.numpy as jnp
from jax import lax
from jax.experimental import pallas as pl
from jax.experimental.pallas import tpu as pltpu
from jax.sharding import PartitionSpec as P

MESH = pl.DeviceIdType.MESH
TILE = 64
TASKS = 8
LANES = 128
PACK = TILE * TILE // LANES
TA = 8
TB = 16
A_COLS = 2048
B_COLS = 1024
OWNED = 24
N_SEND_A = 30
HIGH_BY_CROSS = (0, 1, 2)
LOW_BY_CROSS = (0, 1, 2)
N_LOW_B = 12 + len(HIGH_BY_CROSS) - len(LOW_BY_CROSS)
N_HIGH_B = 12 + len(LOW_BY_CROSS) - len(HIGH_BY_CROSS)
Z_CUTS = ((0, 4), (4, 6), (10, 8), (18, 6))
PEER_CUTS = Z_CUTS + ((24, 24),)


def low_half(rows):
    return lax.broadcasted_iota(jnp.int32, (rows, LANES), 1) < TILE


def kernel(
    a_hbm, b_hbm, ai_hbm, bi_hbm, out_ref,
    a_raw, b_raw, ai, bi, a_wide, b_wide, b_mix, panel_a, panel_b, a_dup, b_dup,
    own_z, own_out, to_peer, from_peer, to_z, from_z, out_wide,
    in_sem, ready, send_a, recv_a, send_b, recv_b, send_p, recv_p, send_z, recv_z,
):
    row = lax.axis_index("row")
    col = lax.axis_index("col")
    layer = lax.axis_index("layer")
    cx, cy = col // 4, col % 4
    zl, core = layer // 2, layer % 2

    def at_x(d):
        return (cx + d) % 4 * 4 + cy

    def at_y(d):
        return cx * 4 + (cy + d) % 4

    def dev(r=row, c=col, l=layer):
        return (r, c, l)

    peer = dev(l=zl * 2 + (1 - core))
    partner = dev(l=(1 - zl) * 2 + core)
    mate, cross, far = row + 1 - 2 * (row % 2), 3 - row, (row + 2) % 4
    is_low = row < 2

    barrier = pltpu.get_barrier_semaphore()

    @pl.when(is_low)
    def _():
        pl.semaphore_signal(barrier, inc=1, device_id=dev(r=cross), device_id_type=MESH)

    friends = [dev(r=mate)] + [dev(c=at(d)) for d in (2, 1, 3) for at in (at_x, at_y)] + [partner, peer]
    for other in friends:
        pl.semaphore_signal(barrier, inc=1, device_id=other, device_id_type=MESH)

    def b_in(c):
        cut = pl.ds(c * B_COLS, B_COLS)
        return pltpu.make_async_copy(b_hbm.at[:, cut], b_raw.at[:, cut], in_sem.at[c])

    def a_in(half):
        cut = pl.ds(half * A_COLS, A_COLS)
        return pltpu.make_async_copy(a_hbm.at[:, cut], a_raw.at[:, cut], in_sem.at[4 + half])

    ai_in = pltpu.make_async_copy(ai_hbm, ai, in_sem.at[6])
    bi_in = pltpu.make_async_copy(bi_hbm, bi, in_sem.at[7])
    for cp in (b_in(0), b_in(3), a_in(0), a_in(1), b_in(1), b_in(2), ai_in, bi_in):
        cp.start()

    low8, low16, low32, low64 = (low_half(n) for n in (8, 16, 32, 64))

    def pack_b(c):
        b_in(c).wait()
        for j in range(8 * c, 8 * c + 8):
            b_wide[pl.ds(j * TB, TB)] = b_raw[:, j * LANES:(j + 1) * LANES].astype(jnp.float32)
        for u in range(8):
            p = b_wide[pl.ds(8 * c * TB + u, 8, stride=TB)]
            q = b_wide[pl.ds(8 * c * TB + u + 8, 8, stride=TB)]
            base = (c * 8 + u) * 16
            b_mix[pl.ds(base, 8, stride=2)] = jnp.where(low8, p, pltpu.roll(q, TILE, 1))
            b_mix[pl.ds(base + 1, 8, stride=2)] = jnp.where(low8, pltpu.roll(p, TILE, 1), q)
        for u in range(8):
            panel_b[row, c, u] = b_mix[pl.ds((c * 8 + u) * 16, 16)].astype(jnp.bfloat16)

    def pack_a(half):
        a_in(half).wait()
        for j in range(16 * half, 16 * half + 16):
            a_wide[pl.ds(j * TA, TA)] = a_raw[:, j * LANES:(j + 1) * LANES].astype(jnp.float32)
        for t in range(TA):
            panel_a[half, col, t] = a_wide[pl.ds(half * 16 * TA + t, 16, stride=TA)].astype(jnp.bfloat16)

    def wait_b(h, c):
        part = panel_b.at[h, c]
        pltpu.make_async_copy(part, part, recv_b.at[h, c]).wait()

    def wait_a(half, g):
        part = panel_a.at[half, g]
        pltpu.make_async_copy(part, part, recv_a.at[half, g]).wait()

    def spread_b(h, c):
        rows = pl.ds(16 * c, 16)
        for u in range(8):
            q = panel_b[h, c, u]
            turned = pltpu.roll(q, TILE, 1)
            b_dup[h * TB + u, rows] = jnp.where(low16, q, turned)
            b_dup[h * TB + 8 + u, rows] = jnp.where(low16, turned, q)

    def spread_a(half, g):
        for t in range(TA):
            q = panel_a[half, g, t]
            turned = pltpu.roll(q, TILE, 1)
            a_dup[g * TA + t, pl.ds(16 * half, 16)] = jnp.where(low16, q, turned)
            a_dup[g * TA + t, pl.ds(32 + 16 * half, 16)] = jnp.where(low16, turned, q)

    def gather(low):
        count = {"a": 0, "b": 0}

        def send(kind, part, ssem, rsem, device):
            pltpu.make_async_remote_copy(
                part, part, ssem.at[count[kind]], rsem, device_id=device, device_id_type=MESH
            ).start()
            count[kind] += 1

        def b_to(r, h, c):
            send("b", panel_b.at[h, c], send_b, recv_b.at[h, c], dev(r=r))

        def along_x(half, g):
            for d in (1, 3, 2):
                send("a", panel_a.at[half, g], send_a, recv_a.at[half, g], dev(c=at_x(d)))

        def along_y(half, g):
            for d in (1, 3, 2):
                send("a", panel_a.at[half, g], send_a, recv_a.at[half, g], dev(c=at_y(d)))

        def pass_on_a(d):
            wait_a(0, at_x(d))
            along_y(0, at_x(d))
            wait_a(1, at_y(d))
            along_x(1, at_y(d))

        def pass_on_b(source, c, r):
            wait_b(source, c)
            b_to(r, source, c)

        def spread_own():
            a_dup[16 * TA] = jnp.zeros((TILE, LANES), jnp.bfloat16)
            for half in range(2):
                spread_a(half, col)
            for c in range(4):
                spread_b(row, c)

        if low:
            pack_a(0)
            pl.semaphore_wait(barrier, len(friends))
            along_x(0, col)
            pack_a(1)
            along_y(1, col)
            for c in (3, 2, 1, 0):
                pack_b(c)
                b_to(mate, row, c)
            along_y(0, col)
            along_x(1, col)
            spread_own()
            for d in (1, 3, 2):
                pass_on_a(d)
            pl.semaphore_wait(ready, 1)
            b_to(cross, row, 0)
            b_to(cross, row, 1)
            pass_on_b(cross, 0, mate)
            b_to(cross, row, 2)
            pass_on_b(cross, 1, mate)
            pass_on_b(mate, 3, cross)
            b_to(cross, row, 3)
            pass_on_b(cross, 2, mate)
        else:
            pack_b(0)
            pl.semaphore_wait(barrier, len(friends) + 1)
            pl.semaphore_signal(ready, inc=1, device_id=dev(r=cross), device_id_type=MESH)
            b_to(cross, row, 0)
            pack_b(3)
            b_to(mate, row, 3)
            pack_b(1)
            b_to(cross, row, 1)
            pack_b(2)
            b_to(cross, row, 2)
            b_to(cross, row, 3)
            pack_a(0)
            along_x(0, col)
            pack_a(1)
            along_y(1, col)
            along_y(0, col)
            along_x(1, col)
            for c in (0, 1, 2):
                b_to(mate, row, c)
            spread_own()
            pass_on_a(1)
            pass_on_a(3)
            for c in range(4):
                if c not in HIGH_BY_CROSS:
                    pass_on_b(mate, c, cross)
            pass_on_a(2)
            for c in LOW_BY_CROSS:
                pass_on_b(cross, c, mate)

    @pl.when(is_low)
    def _():
        gather(True)

    @pl.when(jnp.logical_not(is_low))
    def _():
        gather(False)

    def later(low, source, c):
        passed = HIGH_BY_CROSS if low else LOW_BY_CROSS
        other = LOW_BY_CROSS if low else HIGH_BY_CROSS
        return c not in passed if source == "cross" else c in other

    def last_waits(low):
        for d in (1, 3, 2):
            spread_a(0, at_x(d))
            spread_a(1, at_y(d))

        def rest_of_a(d):
            for e in (0, 1, 3, 2):
                g = (cx + e) % 4 * 4 + (cy + d) % 4
                wait_a(0, g)
                spread_a(0, g)
                g = (cx + d) % 4 * 4 + (cy + e) % 4
                wait_a(1, g)
                spread_a(1, g)

        rest_of_a(1)
        for c in range(4):
            if later(low, "cross", c):
                wait_b(cross, c)
            spread_b(cross, c)
            if later(low, "mate", c):
                wait_b(mate, c)
            spread_b(mate, c)
        rest_of_a(3)
        rest_of_a(2)
        for c in range(4):
            wait_b(far, c)
            spread_b(far, c)

    @pl.when(is_low)
    def _():
        last_waits(True)

    @pl.when(jnp.logical_not(is_low))
    def _():
        last_waits(False)

    ai_in.wait()
    bi_in.wait()

    def product(s):
        left = [
            jnp.where(low64, a_dup[ai[0, s * TASKS + 2 * p]], a_dup[ai[0, s * TASKS + 2 * p + 1]])
            for p in range(TASKS // 2)
        ]
        right = [b_dup[bi[0, s * TASKS + e]] for e in range(TASKS)]
        full = jnp.dot(
            jnp.concatenate(left, axis=1),
            jnp.concatenate(right, axis=0),
            preferred_element_type=jnp.float32,
        )
        return jnp.where(low32, full[:PACK], full[PACK:])

    g1 = ((1 - zl) * 2 + (1 - core)) * OWNED
    g2 = ((1 - zl) * 2 + core) * OWNED
    g3 = (zl * 2 + (1 - core)) * OWNED
    g4 = (zl * 2 + core) * OWNED

    def peer_copy(i):
        first, count = PEER_CUTS[i]
        cut = pl.ds(first, count)
        return pltpu.make_async_remote_copy(
            to_peer.at[cut], from_peer.at[cut], send_p.at[i], recv_p.at[i],
            device_id=peer, device_id_type=MESH,
        )

    def z_copy(i):
        first, count = Z_CUTS[i]
        cut = pl.ds(first, count)
        return pltpu.make_async_remote_copy(
            to_z.at[cut], from_z.at[cut], send_z.at[i], recv_z.at[i],
            device_id=partner, device_id_type=MESH,
        )

    def for_peer(i, base):
        first, count = PEER_CUTS[i]
        for s in range(first, first + count):
            to_peer[s] = product(base + s % OWNED).astype(jnp.bfloat16)
        peer_copy(i).start()

    def for_z(i):
        first, count = Z_CUTS[i]
        for s in range(first, first + count):
            own_z[s] = product(g2 + s)

    def send_on(i):
        first, count = Z_CUTS[i]
        peer_copy(i).wait_recv()
        for s in range(first, first + count):
            to_z[s] = (own_z[s] + from_peer[s].astype(jnp.float32)).astype(jnp.bfloat16)
        z_copy(i).start()

    n_z, n_peer = len(Z_CUTS), len(PEER_CUTS)
    for i in range(n_z):
        for_peer(i, g1)
    for i in range(n_z):
        for_z(i)
        send_on(i)
    for i in range(n_z, n_peer):
        for_peer(i, g3)
    for s in range(OWNED):
        own_out[s] = product(g4 + s)
    for i in range(n_z, n_peer):
        peer_copy(i).wait_recv()
        first, count = PEER_CUTS[i]
        for s in range(first, first + count):
            own_out[s - OWNED] += from_peer[s].astype(jnp.float32)
    for i in range(N_SEND_A):
        pltpu.make_async_copy(panel_a.at[0, 0], panel_a.at[0, 0], send_a.at[i]).wait()
    def b_sent(first, last):
        for i in range(first, last):
            pltpu.make_async_copy(panel_b.at[0, 0], panel_b.at[0, 0], send_b.at[i]).wait()

    @pl.when(is_low)
    def _():
        b_sent(0, N_LOW_B)

    @pl.when(jnp.logical_not(is_low))
    def _():
        b_sent(0, N_HIGH_B)

    for i in range(n_peer):
        peer_copy(i).wait_send()
    for i in range(n_z):
        first, count = Z_CUTS[i]
        z_copy(i).wait_recv()
        for s in range(first, first + count):
            out_wide[pl.ds(s, PACK, stride=OWNED)] = own_out[s] + from_z[s].astype(jnp.float32)
    for j in range(PACK):
        out_ref[:, j * LANES:(j + 1) * LANES] = out_wide[pl.ds(j * OWNED, OWNED)].astype(jnp.bfloat16)

    for i in range(n_z):
        z_copy(i).wait_send()


def shards(a_tiles, b_tiles, a_slots, b_slots):
    flat = TILE * TILE
    bf16, f32 = jnp.bfloat16, jnp.float32
    out = pl.pallas_call(
        kernel,
        out_shape=pltpu.VMEM((OWNED, flat), bf16),
        in_specs=[pl.BlockSpec(memory_space=pl.ANY)] * 4,
        out_specs=pl.BlockSpec(memory_space=pltpu.VMEM),
        scratch_shapes=[
            pltpu.VMEM((TA, flat), bf16),
            pltpu.VMEM((TB, flat), bf16),
            pltpu.SMEM((1, 768), jnp.int32),
            pltpu.SMEM((1, 768), jnp.int32),
            pltpu.VMEM((TA * PACK, LANES), f32),
            pltpu.VMEM((TB * PACK, LANES), f32),
            pltpu.VMEM((TB * PACK, LANES), f32),
            pltpu.VMEM((2, 16, TA, 16, LANES), bf16),
            pltpu.VMEM((4, 4, TB // 2, 16, LANES), bf16),
            pltpu.VMEM((16 * TA + 1, TILE, LANES), bf16),
            pltpu.VMEM((4 * TB, TILE, LANES), bf16),
            pltpu.VMEM((OWNED, PACK, LANES), f32),
            pltpu.VMEM((OWNED, PACK, LANES), f32),
            pltpu.VMEM((2 * OWNED, PACK, LANES), bf16),
            pltpu.VMEM((2 * OWNED, PACK, LANES), bf16),
            pltpu.VMEM((OWNED, PACK, LANES), bf16),
            pltpu.VMEM((OWNED, PACK, LANES), bf16),
            pltpu.VMEM((PACK * OWNED, LANES), f32),
            pltpu.SemaphoreType.DMA((8,)),
            pltpu.SemaphoreType.REGULAR,
            pltpu.SemaphoreType.DMA((N_SEND_A,)),
            pltpu.SemaphoreType.DMA((2, 16)),
            pltpu.SemaphoreType.DMA((16,)),
            pltpu.SemaphoreType.DMA((4, 4)),
            pltpu.SemaphoreType.DMA((len(PEER_CUTS),)),
            pltpu.SemaphoreType.DMA((len(PEER_CUTS),)),
            pltpu.SemaphoreType.DMA((len(Z_CUTS),)),
            pltpu.SemaphoreType.DMA((len(Z_CUTS),)),
        ],
        compiler_params=pltpu.CompilerParams(
            collective_id=0, has_side_effects=True, vmem_limit_bytes=60 * 2**20
        ),
        name="purify",
    )(
        a_tiles.reshape(TA, flat), b_tiles.reshape(TB, flat),
        a_slots.reshape(1, -1), b_slots.reshape(1, -1),
    )
    return out.reshape(1, 1, OWNED, flat)


def solution(mesh):
    in_specs = (
        P("row", "layer", "col", None, None),
        P("layer", "row", "col", None, None),
        P("row", "col", "layer", None),
        P("row", "col", "layer", None),
    )
    out_specs = P("row", "col", "layer", None)
    return jax.shard_map(shards, mesh=mesh, in_specs=in_specs, out_specs=out_specs, check_vma=False)
```

```python
import jax
import jax.numpy as jnp
from jax import lax
from jax.experimental import pallas as pl
from jax.experimental.pallas import tpu as pltpu
from jax.sharding import PartitionSpec as P

MESH = pl.DeviceIdType.MESH
TILE = 64
TASKS = 8
LANES = 128
PACK = TILE * TILE // LANES
TA = 8
TB = 16
A_COLS = 2048
B_COLS = 1024
OWNED = 24
N_SEND_A = 30
LOW_BY_CROSS = (0, 1, 2)
N_B = 11
SPARE = 12
Z_CUTS = ((0, 4), (4, 4), (8, 4), (12, 4), (16, 4), (20, 4))
PEER_CUTS = Z_CUTS + ((24, 24),)


def low_half(rows):
    return lax.broadcasted_iota(jnp.int32, (rows, LANES), 1) < TILE


def kernel(
    a_hbm, b_hbm, ai_hbm, bi_hbm, out_ref,
    a_raw, b_raw, ai, bi, a_wide, b_wide, b_mix, panel_a, panel_b, a_dup, b_dup,
    own_z, own_out, to_peer, from_peer, to_z, from_z, out_wide,
    in_sem, ready, send_a, recv_a, send_b, recv_b, send_p, recv_p, send_z, recv_z,
):
    row = lax.axis_index("row")
    col = lax.axis_index("col")
    layer = lax.axis_index("layer")
    cx, cy = col // 4, col % 4
    zl, core = layer // 2, layer % 2

    def at_x(d):
        return (cx + d) % 4 * 4 + cy

    def at_y(d):
        return cx * 4 + (cy + d) % 4

    def dev(r=row, c=col, l=layer):
        return (r, c, l)

    peer = dev(l=zl * 2 + (1 - core))
    partner = dev(l=(1 - zl) * 2 + core)
    mate, cross, far = row + 1 - 2 * (row % 2), 3 - row, (row + 2) % 4
    is_low = row < 2
    mate_outer = zl == mate % 2

    barrier = pltpu.get_barrier_semaphore()

    @pl.when(is_low)
    def _():
        pl.semaphore_signal(barrier, inc=1, device_id=dev(r=cross), device_id_type=MESH)

    friends = [dev(r=mate)] + [dev(c=at(d)) for d in (2, 1, 3) for at in (at_x, at_y)] + [partner, peer]
    for other in friends:
        pl.semaphore_signal(barrier, inc=1, device_id=other, device_id_type=MESH)

    def b_in(c):
        cut = pl.ds(c * B_COLS, B_COLS)
        return pltpu.make_async_copy(b_hbm.at[:, cut], b_raw.at[:, cut], in_sem.at[c])

    def a_in(half):
        cut = pl.ds(half * A_COLS, A_COLS)
        return pltpu.make_async_copy(a_hbm.at[:, cut], a_raw.at[:, cut], in_sem.at[4 + half])

    ai_in = pltpu.make_async_copy(ai_hbm, ai, in_sem.at[6])
    bi_in = pltpu.make_async_copy(bi_hbm, bi, in_sem.at[7])
    for cp in (b_in(0), b_in(3), a_in(0), a_in(1), b_in(1), b_in(2), ai_in, bi_in):
        cp.start()

    low8, low16, low32, low64 = (low_half(n) for n in (8, 16, 32, 64))

    def pack_b(c):
        b_in(c).wait()
        for j in range(8 * c, 8 * c + 8):
            b_wide[pl.ds(j * TB, TB)] = b_raw[:, j * LANES:(j + 1) * LANES].astype(jnp.float32)
        for u in range(8):
            p = b_wide[pl.ds(8 * c * TB + u, 8, stride=TB)]
            q = b_wide[pl.ds(8 * c * TB + u + 8, 8, stride=TB)]
            base = (c * 8 + u) * 16
            b_mix[pl.ds(base, 8, stride=2)] = jnp.where(low8, p, pltpu.roll(q, TILE, 1))
            b_mix[pl.ds(base + 1, 8, stride=2)] = jnp.where(low8, pltpu.roll(p, TILE, 1), q)
        for u in range(8):
            panel_b[row, c, u] = b_mix[pl.ds((c * 8 + u) * 16, 16)].astype(jnp.bfloat16)

    def pack_a(half):
        a_in(half).wait()
        for j in range(16 * half, 16 * half + 16):
            a_wide[pl.ds(j * TA, TA)] = a_raw[:, j * LANES:(j + 1) * LANES].astype(jnp.float32)
        for t in range(TA):
            panel_a[half, col, t] = a_wide[pl.ds(half * 16 * TA + t, 16, stride=TA)].astype(jnp.bfloat16)

    def wait_b(h, c):
        part = panel_b.at[h, c]
        pltpu.make_async_copy(part, part, recv_b.at[h, c]).wait()

    def wait_a(half, g):
        part = panel_a.at[half, g]
        pltpu.make_async_copy(part, part, recv_a.at[half, g]).wait()

    def spread_b(h, c):
        rows = pl.ds(16 * c, 16)
        for u in range(8):
            q = panel_b[h, c, u]
            turned = pltpu.roll(q, TILE, 1)
            b_dup[h * TB + u, rows] = jnp.where(low16, q, turned)
            b_dup[h * TB + 8 + u, rows] = jnp.where(low16, turned, q)

    def spread_a(half, g):
        for t in range(TA):
            q = panel_a[half, g, t]
            turned = pltpu.roll(q, TILE, 1)
            a_dup[g * TA + t, pl.ds(16 * half, 16)] = jnp.where(low16, q, turned)
            a_dup[g * TA + t, pl.ds(32 + 16 * half, 16)] = jnp.where(low16, turned, q)

    def gather(low):
        count = {"a": 0, "b": 0}

        def send(kind, part, ssem, rsem, device):
            pltpu.make_async_remote_copy(
                part, part, ssem.at[count[kind]], rsem, device_id=device, device_id_type=MESH
            ).start()
            count[kind] += 1

        def b_to(r, h, c):
            send("b", panel_b.at[h, c], send_b, recv_b.at[h, c], dev(r=r))

        def along_x(half, g):
            for d in (1, 3, 2):
                send("a", panel_a.at[half, g], send_a, recv_a.at[half, g], dev(c=at_x(d)))

        def along_y(half, g):
            for d in (1, 3, 2):
                send("a", panel_a.at[half, g], send_a, recv_a.at[half, g], dev(c=at_y(d)))

        def pass_on_a(d):
            wait_a(0, at_x(d))
            along_y(0, at_x(d))
            wait_a(1, at_y(d))
            along_x(1, at_y(d))

        def spare(source, c, r):
            part = panel_b.at[source, c]
            pltpu.make_async_remote_copy(
                part, part, send_b.at[SPARE], recv_b.at[source, c], device_id=dev(r=r), device_id_type=MESH
            ).start()

        def pass_on_b(source, c, r):
            wait_b(source, c)
            b_to(r, source, c)

        def spread_own():
            a_dup[16 * TA] = jnp.zeros((TILE, LANES), jnp.bfloat16)
            for half in range(2):
                spread_a(half, col)
            for c in range(4):
                spread_b(row, c)

        if low:
            pack_a(0)
            pl.semaphore_wait(barrier, len(friends))
            along_x(0, col)
            pack_a(1)
            along_y(1, col)
            for c in (3, 2, 1, 0):
                pack_b(c)
                b_to(mate, row, c)
            along_y(0, col)
            along_x(1, col)
            spread_own()
            for d in (1, 3, 2):
                pass_on_a(d)
            pl.semaphore_wait(ready, 1)
            for c in range(4):
                b_to(cross, row, c)
                if c not in LOW_BY_CROSS:
                    pass_on_b(mate, c, cross)
            for c in (0, 1):
                pass_on_b(cross, c, mate)
            wait_b(cross, 2)

            @pl.when(mate_outer)
            def _():
                spare(cross, 2, mate)
        else:
            pack_b(0)
            pl.semaphore_wait(barrier, len(friends) + 1)
            pl.semaphore_signal(ready, inc=1, device_id=dev(r=cross), device_id_type=MESH)
            b_to(cross, row, 0)
            pack_b(3)
            b_to(mate, row, 3)
            pack_b(1)
            b_to(cross, row, 1)
            pack_b(2)
            b_to(cross, row, 2)
            b_to(mate, row, 2)
            b_to(cross, row, 3)
            pack_a(0)
            along_x(0, col)
            pack_a(1)
            along_y(1, col)
            along_y(0, col)
            along_x(1, col)
            for c in (0, 1):
                b_to(mate, row, c)
            spread_own()
            pass_on_a(1)
            pass_on_a(3)
            pass_on_b(mate, 3, cross)
            wait_b(mate, 2)

            @pl.when(jnp.logical_not(mate_outer))
            def _():
                spare(mate, 2, cross)

            pass_on_a(2)
            for c in LOW_BY_CROSS:
                pass_on_b(cross, c, mate)

    @pl.when(is_low)
    def _():
        gather(True)

    @pl.when(jnp.logical_not(is_low))
    def _():
        gather(False)

    def later(low, source, c):
        if source == "cross":
            return c == 3
        return c < 3 if low else c < 2

    def last_waits(low):
        for d in (1, 3, 2):
            spread_a(0, at_x(d))
            spread_a(1, at_y(d))

        def rest_of_a(d):
            for e in (0, 1, 3, 2):
                g = (cx + e) % 4 * 4 + (cy + d) % 4
                wait_a(0, g)
                spread_a(0, g)
                g = (cx + d) % 4 * 4 + (cy + e) % 4
                wait_a(1, g)
                spread_a(1, g)

        rest_of_a(1)
        for c in range(4):
            if later(low, "cross", c):
                wait_b(cross, c)
            spread_b(cross, c)
            if later(low, "mate", c):
                wait_b(mate, c)
            spread_b(mate, c)
        rest_of_a(3)
        rest_of_a(2)
        for c in range(4):
            wait_b(far, c)
            spread_b(far, c)

    @pl.when(is_low)
    def _():
        last_waits(True)

    @pl.when(jnp.logical_not(is_low))
    def _():
        last_waits(False)

    ai_in.wait()
    bi_in.wait()

    def product(s):
        left = [
            jnp.where(low64, a_dup[ai[0, s * TASKS + 2 * p]], a_dup[ai[0, s * TASKS + 2 * p + 1]])
            for p in range(TASKS // 2)
        ]
        right = [b_dup[bi[0, s * TASKS + e]] for e in range(TASKS)]
        full = jnp.dot(
            jnp.concatenate(left, axis=1),
            jnp.concatenate(right, axis=0),
            preferred_element_type=jnp.float32,
        )
        return jnp.where(low32, full[:PACK], full[PACK:])

    g1 = ((1 - zl) * 2 + (1 - core)) * OWNED
    g2 = ((1 - zl) * 2 + core) * OWNED
    g3 = (zl * 2 + (1 - core)) * OWNED
    g4 = (zl * 2 + core) * OWNED

    def peer_copy(i):
        first, count = PEER_CUTS[i]
        cut = pl.ds(first, count)
        return pltpu.make_async_remote_copy(
            to_peer.at[cut], from_peer.at[cut], send_p.at[i], recv_p.at[i],
            device_id=peer, device_id_type=MESH,
        )

    def z_copy(i):
        first, count = Z_CUTS[i]
        cut = pl.ds(first, count)
        return pltpu.make_async_remote_copy(
            to_z.at[cut], from_z.at[cut], send_z.at[i], recv_z.at[i],
            device_id=partner, device_id_type=MESH,
        )

    def for_peer(i, base):
        first, count = PEER_CUTS[i]
        for s in range(first, first + count):
            to_peer[s] = product(base + s % OWNED).astype(jnp.bfloat16)
        peer_copy(i).start()

    def for_z(i):
        first, count = Z_CUTS[i]
        for s in range(first, first + count):
            own_z[s] = product(g2 + s)

    def send_on(i):
        first, count = Z_CUTS[i]
        peer_copy(i).wait_recv()
        for s in range(first, first + count):
            to_z[s] = (own_z[s] + from_peer[s].astype(jnp.float32)).astype(jnp.bfloat16)
        z_copy(i).start()

    n_z, n_peer = len(Z_CUTS), len(PEER_CUTS)
    for i in range(n_z):
        for_peer(i, g1)
    for i in range(n_z):
        for_z(i)
        send_on(i)
    for i in range(n_z, n_peer):
        for_peer(i, g3)
    for s in range(OWNED):
        own_out[s] = product(g4 + s)
    for i in range(n_z, n_peer):
        peer_copy(i).wait_recv()
        first, count = PEER_CUTS[i]
        for s in range(first, first + count):
            own_out[s - OWNED] += from_peer[s].astype(jnp.float32)
    for i in range(N_SEND_A):
        pltpu.make_async_copy(panel_a.at[0, 0], panel_a.at[0, 0], send_a.at[i]).wait()
    def b_sent(first, last):
        for i in range(first, last):
            pltpu.make_async_copy(panel_b.at[0, 0], panel_b.at[0, 0], send_b.at[i]).wait()

    b_sent(0, N_B)

    @pl.when(jnp.logical_not(is_low))
    def _():
        b_sent(N_B, SPARE)

    @pl.when(is_low == mate_outer)
    def _():
        b_sent(SPARE, SPARE + 1)

    for i in range(n_peer):
        peer_copy(i).wait_send()
    for i in range(n_z):
        first, count = Z_CUTS[i]
        z_copy(i).wait_recv()
        for s in range(first, first + count):
            out_wide[pl.ds(s, PACK, stride=OWNED)] = own_out[s] + from_z[s].astype(jnp.float32)
    for j in range(PACK):
        out_ref[:, j * LANES:(j + 1) * LANES] = out_wide[pl.ds(j * OWNED, OWNED)].astype(jnp.bfloat16)

    for i in range(n_z):
        z_copy(i).wait_send()


def shards(a_tiles, b_tiles, a_slots, b_slots):
    flat = TILE * TILE
    bf16, f32 = jnp.bfloat16, jnp.float32
    out = pl.pallas_call(
        kernel,
        out_shape=pltpu.VMEM((OWNED, flat), bf16),
        in_specs=[pl.BlockSpec(memory_space=pl.ANY)] * 4,
        out_specs=pl.BlockSpec(memory_space=pltpu.VMEM),
        scratch_shapes=[
            pltpu.VMEM((TA, flat), bf16),
            pltpu.VMEM((TB, flat), bf16),
            pltpu.SMEM((1, 768), jnp.int32),
            pltpu.SMEM((1, 768), jnp.int32),
            pltpu.VMEM((TA * PACK, LANES), f32),
            pltpu.VMEM((TB * PACK, LANES), f32),
            pltpu.VMEM((TB * PACK, LANES), f32),
            pltpu.VMEM((2, 16, TA, 16, LANES), bf16),
            pltpu.VMEM((4, 4, TB // 2, 16, LANES), bf16),
            pltpu.VMEM((16 * TA + 1, TILE, LANES), bf16),
            pltpu.VMEM((4 * TB, TILE, LANES), bf16),
            pltpu.VMEM((OWNED, PACK, LANES), f32),
            pltpu.VMEM((OWNED, PACK, LANES), f32),
            pltpu.VMEM((2 * OWNED, PACK, LANES), bf16),
            pltpu.VMEM((2 * OWNED, PACK, LANES), bf16),
            pltpu.VMEM((OWNED, PACK, LANES), bf16),
            pltpu.VMEM((OWNED, PACK, LANES), bf16),
            pltpu.VMEM((PACK * OWNED, LANES), f32),
            pltpu.SemaphoreType.DMA((8,)),
            pltpu.SemaphoreType.REGULAR,
            pltpu.SemaphoreType.DMA((N_SEND_A,)),
            pltpu.SemaphoreType.DMA((2, 16)),
            pltpu.SemaphoreType.DMA((SPARE + 1,)),
            pltpu.SemaphoreType.DMA((4, 4)),
            pltpu.SemaphoreType.DMA((len(PEER_CUTS),)),
            pltpu.SemaphoreType.DMA((len(PEER_CUTS),)),
            pltpu.SemaphoreType.DMA((len(Z_CUTS),)),
            pltpu.SemaphoreType.DMA((len(Z_CUTS),)),
        ],
        compiler_params=pltpu.CompilerParams(
            collective_id=0, has_side_effects=True, vmem_limit_bytes=60 * 2**20
        ),
        name="purify",
    )(
        a_tiles.reshape(TA, flat), b_tiles.reshape(TB, flat),
        a_slots.reshape(1, -1), b_slots.reshape(1, -1),
    )
    return out.reshape(1, 1, OWNED, flat)


def solution(mesh):
    in_specs = (
        P("row", "layer", "col", None, None),
        P("layer", "row", "col", None, None),
        P("row", "col", "layer", None),
        P("row", "col", "layer", None),
    )
    out_specs = P("row", "col", "layer", None)
    return jax.shard_map(shards, mesh=mesh, in_specs=in_specs, out_specs=out_specs, check_vma=False)
```
